32 devices in a mesh: groups: 2 (over y), wide: 4 (over z), short: 2 (over x), sub: 2 (over core).
Axes of the slice: x: 2, y: 2, z: 4, core: 2. Of those that a mesh axis runs over, the one named last changes fastest.
Arguments:
- residual: bfloat16 [8, 12288], P('groups', 'wide'), parts along dimension 0, may hold values from -21 to 21
- attn_gain: bfloat16 [12288], P('wide'), may hold values from 0.099609375 to 1.8984375
- query_weight: bfloat16 [12288, 6144], P('wide', ('short', 'sub')), may hold values from -3 to 3
- key_value_weight: bfloat16 [12288, 1024], P('wide', ('short', 'sub')), may hold values from -3 to 3
- output_weight: bfloat16 [6144, 12288], P('short', ('wide', 'sub')), may hold values from -0.078125 to 0.078125
- cache_keys: bfloat16 [8, 4, 2048, 128], P('groups', 'short', ('wide', 'sub')), parts along dimension 0, may hold values from -16 to 16
- cached_value_rows: bfloat16 [8, 4, 2048, 128], P('groups', 'short', ('wide', 'sub')), parts along dimension 0, may hold values from -6 to 6
- lengths: int32 [8], P('groups'), parts along dimension 0, may hold values from 1024 to 2048, as said below
- positions: int32 [8], P('groups'), parts along dimension 0, may hold values from 2048 to 4095
- ffn_gain: bfloat16 [12288], P(('wide', 'sub')), may hold values from 0.099609375 to 1.8984375
- gate_weight: bfloat16 [12288, 14336], P(('wide', 'sub'), 'short'), may hold values from -0.0546875 to 0.0546875
- up_weight: bfloat16 [12288, 14336], P(('wide', 'sub'), 'short'), may hold values from -0.0546875 to 0.0546875
- down_weight: bfloat16 [14336, 12288], P('short', ('wide', 'sub')), may hold values from -0.046875 to 0.046875
Outputs:
- layer_out: bfloat16 [8, 12288], P('groups', ('wide', 'sub')), parts along dimension 0
The draws below stay inside these ranges and needn't reach their ends.
There are 2 independent parts, one for each index of `groups`. The reference program is written for one: setup_inputs(seed, part) draws one part's arguments, and reference() takes and returns one part's arrays. A program takes and returns all parts, laid end to end along the dimension named above; an argument that names none is the same for every part. Nothing has to cross between parts.
Inputs may be any that keep to these rules, and one draw needn't show every extreme that they name: `lengths`: in every draw some answer has all 2048 rows cached.
All inputs are finite; a program needn't handle non-finite values.
Results may differ from the reference program's by a relative error of at most 0.008.
Values may be sent and summed in bfloat16 or wider, within the bound.
A program may use at most 128 MiB of HBM per device.

```python
import math
import jax
import jax.numpy as jnp
from jax import lax

MODEL_WIDTH = 12288
FF = 14336
QUERY_HEADS = 48
KEY_HEADS = 4
HEAD_WIDTH = 128
ANSWER_COUNT = 4
CACHE_ROWS = 2048


def draw_residual(key, part):
    first_part, second_part = jax.random.split(jax.random.fold_in(key, 11), 2)
    columns = jnp.exp(math.log(3.0) * (jnp.arange(MODEL_WIDTH, dtype=jnp.float32) / (MODEL_WIDTH - 1) - 0.5))
    base_value = jnp.clip(jax.random.normal(first_part, (ANSWER_COUNT, MODEL_WIDTH), jnp.float32), -4.0, 4.0)
    scales = jnp.exp(jax.random.uniform(second_part, (ANSWER_COUNT, 1), jnp.float32, math.log(0.5), math.log(2.0)))
    return jnp.clip(base_value * scales * columns[None, :], -21.0, 21.0).astype(jnp.bfloat16)


def query_base(key):
    first_part = jax.random.fold_in(jax.random.fold_in(key, 31), 0)
    base_value = jnp.clip(jax.random.normal(first_part, (MODEL_WIDTH, QUERY_HEADS, HEAD_WIDTH), jnp.float32), -4.0, 4.0) / math.sqrt(MODEL_WIDTH)
    return base_value


def draw_query_weight(key, part):
    return query_base(key).reshape(MODEL_WIDTH, QUERY_HEADS * HEAD_WIDTH).astype(jnp.bfloat16)


def draw_key_value_weight(key, part):
    first_part = jax.random.fold_in(jax.random.fold_in(key, 43), 0)
    base_value = jnp.clip(jax.random.normal(first_part, (MODEL_WIDTH, KEY_HEADS, 2, HEAD_WIDTH), jnp.float32), -4.0, 4.0) / math.sqrt(MODEL_WIDTH)
    return jnp.clip(base_value, -3.0, 3.0).reshape(MODEL_WIDTH, 2 * KEY_HEADS * HEAD_WIDTH).astype(jnp.bfloat16)


def draw_cache_keys(key, part):
    first_part = jax.random.fold_in(jax.random.fold_in(key, 23), 0)
    base_value = jnp.clip(jax.random.normal(first_part, (ANSWER_COUNT, KEY_HEADS, CACHE_ROWS, HEAD_WIDTH), jnp.float32), -4.0, 4.0)
    return base_value.astype(jnp.bfloat16)


def draw_lengths(key, part):
    first_part, second_part = jax.random.split(jax.random.fold_in(key, 7))
    drawn = jax.random.randint(first_part, (ANSWER_COUNT,), CACHE_ROWS // 2, CACHE_ROWS + 1, dtype=jnp.int32)
    chosen = jax.random.randint(second_part, (), 0, ANSWER_COUNT, dtype=jnp.int32)
    return jnp.where(jnp.arange(ANSWER_COUNT, dtype=jnp.int32) == chosen, CACHE_ROWS, drawn).astype(jnp.int32)


def place_ends(values, stream_key, least, top_value):
    dims = values.shape
    spot = [jax.random.randint(jax.random.fold_in(stream_key, axis), (), 0, dims[axis]) for axis in range(len(dims))]
    values = values.at[tuple(spot)].set(least)
    longest = dims.index(max(dims))
    spot[longest] = (spot[longest] + 1) % dims[longest]
    return values.at[tuple(spot)].set(top_value)


def block_levels(key, dims, pieces, smallest, high):
    gain = 1.0
    for position, shards_of in pieces:
        steps = jax.random.uniform(jax.random.fold_in(jax.random.fold_in(key, 6), position), (shards_of,), jnp.float32, smallest / len(pieces), high / len(pieces))
        gain = gain * jnp.repeat(jnp.exp(steps), dims[position] // shards_of).reshape((-1,) + (1,) * (len(dims) - 1 - position))
    return gain


def normal_values(stream_key, dims, width, bound, pieces=(), held_as=jnp.bfloat16):
    gain = block_levels(stream_key, dims, pieces, -0.22, 0.18) if pieces else 1.0
    entries = jax.random.normal(stream_key, dims, jnp.float32) * width * gain
    return jnp.minimum(jnp.maximum(entries, -bound), bound).astype(held_as)


def setup_inputs(seed: int = 0, part: int = 0) -> dict:
    streams_of = jax.random.split(jax.random.key(seed), 14)
    part_splits = jax.random.split(jax.random.fold_in(streams_of[13], part), 14)
    residual = draw_residual(jax.random.fold_in(jax.random.fold_in(streams_of[13], part), 71), part)
    attn_gain = jnp.clip(1.0 + 0.18 * jax.random.normal(streams_of[1], (MODEL_WIDTH,), jnp.float32), 0.099609375, 1.8984375).astype(jnp.bfloat16)
    query_weight = draw_query_weight(jax.random.fold_in(streams_of[13], 71), part)
    key_value_weight = draw_key_value_weight(jax.random.fold_in(streams_of[13], 71), part)
    output_weight = normal_values(streams_of[4], (QUERY_HEADS * HEAD_WIDTH, MODEL_WIDTH), (QUERY_HEADS * HEAD_WIDTH) ** -0.5, 0.078125, ((0, 2), (1, 8)))
    cache_keys = draw_cache_keys(jax.random.fold_in(jax.random.fold_in(streams_of[13], part), 71), part)
    cached_value_rows = normal_values(part_splits[6], (ANSWER_COUNT, KEY_HEADS, CACHE_ROWS, HEAD_WIDTH), 1.0, 6.0, ((1, 2), (2, 8)))
    lengths = draw_lengths(jax.random.fold_in(jax.random.fold_in(streams_of[13], part), 71), part)
    positions = place_ends(jax.random.randint(part_splits[8], (ANSWER_COUNT,), CACHE_ROWS, 2 * CACHE_ROWS), jax.random.fold_in(part_splits[8], 1), CACHE_ROWS, (2 * CACHE_ROWS) - 1).astype(jnp.int32)
    ffn_gain = jnp.clip(1.0 + 0.18 * jax.random.normal(streams_of[9], (MODEL_WIDTH,), jnp.float32), 0.099609375, 1.8984375).astype(jnp.bfloat16)
    gate_weight = normal_values(streams_of[10], (MODEL_WIDTH, FF), MODEL_WIDTH ** -0.5, 0.0546875, ((0, 8), (1, 2)))
    up_weight = normal_values(streams_of[11], (MODEL_WIDTH, FF), MODEL_WIDTH ** -0.5, 0.0546875, ((0, 8), (1, 2)))
    down_weight = normal_values(streams_of[12], (FF, MODEL_WIDTH), FF ** -0.5, 0.046875, ((0, 2), (1, 8)))
    return dict(residual=residual, attn_gain=attn_gain, query_weight=query_weight, key_value_weight=key_value_weight, output_weight=output_weight, cache_keys=cache_keys, cached_value_rows=cached_value_rows, lengths=lengths, positions=positions, ffn_gain=ffn_gain, gate_weight=gate_weight, up_weight=up_weight, down_weight=down_weight)


rope_base = 1000000.0
epsilon = 1e-05
neg_large = -1e+30

def rotate(values, positions):
    half = values.shape[-1] // 2
    freq = rope_base ** (-(jnp.arange(half, dtype=jnp.float32) * 2.0) / values.shape[-1])
    angle = positions.astype(jnp.float32)[:, None] * freq[None, :]
    cosine = jnp.cos(angle)[:, None, :]
    sine = jnp.sin(angle)[:, None, :]
    first_part = values[..., :half]
    second_part = values[..., half:]
    return jnp.concatenate([first_part * cosine - second_part * sine, second_part * cosine + first_part * sine], axis=-1)

def reference(residual, attn_gain, query_weight, key_value_weight, output_weight, cache_keys, cached_value_rows, lengths, positions, ffn_gain, gate_weight, up_weight, down_weight):
    resid = residual.astype(jnp.float32)
    factor = lax.rsqrt(lax.optimization_barrier(jnp.sum(resid * resid, axis=1)) / MODEL_WIDTH + epsilon)[:, None]
    normed = (resid * attn_gain.astype(jnp.float32)).astype(jnp.bfloat16)
    query_rows = factor * jnp.dot(normed, query_weight, preferred_element_type=jnp.float32)
    key_value_rows = factor * jnp.dot(normed, key_value_weight, preferred_element_type=jnp.float32)
    query_rows = rotate(query_rows.reshape(ANSWER_COUNT, QUERY_HEADS, HEAD_WIDTH), positions).astype(jnp.bfloat16)
    key_value_rows = key_value_rows.reshape(ANSWER_COUNT, KEY_HEADS, 2, HEAD_WIDTH)
    new_keys = rotate(key_value_rows[:, :, 0], positions).astype(jnp.bfloat16)
    new_values = key_value_rows[:, :, 1].astype(jnp.bfloat16)
    group_index = QUERY_HEADS // KEY_HEADS
    grouped_rows = query_rows.astype(jnp.float32).reshape(ANSWER_COUNT, KEY_HEADS, group_index, HEAD_WIDTH)
    scaling = 1.0 / math.sqrt(HEAD_WIDTH)
    scores = jnp.einsum('bhgd,bhtd->bhgt', grouped_rows, cache_keys.astype(jnp.float32), precision=lax.Precision.HIGHEST) * scaling
    valid = (jnp.arange(CACHE_ROWS, dtype=jnp.int32)[None, :] < lengths[:, None])[:, None, None, :]
    scores = jnp.where(valid, scores, neg_large)
    own = lax.optimization_barrier(jnp.sum(grouped_rows * new_keys.astype(jnp.float32)[:, :, None, :], axis=-1)) * scaling
    highest = jnp.maximum(lax.optimization_barrier(jnp.max(scores, axis=-1)), own)
    weights = jnp.where(valid, jnp.exp(scores - highest[..., None]), 0.0).astype(jnp.bfloat16)
    own_weight = jnp.exp(own - highest)
    totals = lax.optimization_barrier(jnp.sum(weights.astype(jnp.float32), axis=-1)) + own_weight
    mixed = jnp.einsum('bhgt,bhtd->bhgd', weights.astype(jnp.float32), cached_value_rows.astype(jnp.float32), precision=lax.Precision.HIGHEST)
    mixed = mixed + own_weight[..., None] * new_values.astype(jnp.float32)[:, :, None, :]
    attended = (mixed / totals[..., None]).reshape(ANSWER_COUNT, QUERY_HEADS * HEAD_WIDTH).astype(jnp.bfloat16)
    hidden = resid + jnp.dot(attended, output_weight, preferred_element_type=jnp.float32)
    factor2 = lax.rsqrt(lax.optimization_barrier(jnp.sum(hidden * hidden, axis=1)) / MODEL_WIDTH + epsilon)[:, None]
    normed2 = (hidden * ffn_gain.astype(jnp.float32)).astype(jnp.bfloat16)
    gate = factor2 * jnp.dot(normed2, gate_weight, preferred_element_type=jnp.float32)
    upward = factor2 * jnp.dot(normed2, up_weight, preferred_element_type=jnp.float32)
    activated = (jax.nn.silu(gate) * upward).astype(jnp.bfloat16)
    return (hidden + jnp.dot(activated, down_weight, preferred_element_type=jnp.float32)).astype(jnp.bfloat16)
```

```python
import functools
import math

import jax
import jax.numpy as jnp
from jax import lax
from jax.experimental import pallas as pl
from jax.experimental.pallas import tpu as pltpu
from jax.sharding import PartitionSpec as P

rope_base = 1000000.0
epsilon = 1e-05
neg_large = -1e30
lane = 128
bf16 = jnp.bfloat16
f32 = jnp.float32
weight_budget = 60 * 2**20
vmem_limit = 63 * 2**20


def split_two(value):
    high = value.astype(bf16).astype(f32)
    return high, value - high


def largest_divisor(count, most):
    return max(d for d in range(1, most + 1) if count % d == 0)


class Plan:
    def __init__(self, sizes, residual, query, keyval, output, cache, gate, down):
        self.wide, self.short, self.sub = sizes
        self.members = self.wide * self.sub
        self.answers, self.width = residual
        self.groups = 16 // self.answers
        self.model = self.width * self.wide
        self.query_cols = query[1]
        self.heads = self.query_cols // lane
        self.blocks = keyval[1] // lane
        self.head_tiles = -(-self.heads // self.groups)
        self.pack_cols = -(-(self.heads + self.blocks + 2) // self.groups) * lane
        self.kv_heads = cache[1]
        self.rows = cache[2]
        self.units = self.sub * self.head_tiles
        self.out_rows, self.out_cols = output
        self.gate_rows, self.ff = gate
        self.owners = largest_divisor(self.ff // lane, self.members)
        self.piece = self.ff // self.owners
        self.tiles = self.piece // lane
        self.half = -(-(self.tiles + 1) // self.groups) * lane
        self.query_chunks = largest_divisor(self.width // lane, 6)
        self.out_chunks = largest_divisor(self.out_rows // lane, 6)
        fixed = 2 * (
            query[0] * query[1] + keyval[0] * keyval[1] + output[0] * output[1]
            + 2 * math.prod(cache)
        )
        slot = 2 * self.gate_rows * 2 * self.piece
        self.slots = min(self.members, (weight_budget - fixed) // slot)
        in_query = self.width // self.piece if self.query_cols >= self.out_cols else 0
        in_out = self.out_rows // self.piece
        places = [("query", k) for k in range(in_query)] + [("out", k) for k in range(in_out)]
        places = places[: self.members]
        left = self.members - len(places)
        fits = self.piece <= self.gate_rows and self.out_cols <= 2 * self.piece
        kind = "slot" if fits and left <= self.slots else "extra"
        places += [(kind, k) for k in range(left)]
        self.places = places
        self.extra = max(left * self.piece, 16) if kind == "extra" else 16
        assert self.units <= self.members and self.sub % self.kv_heads == 0
        assert self.blocks * self.sub == 2 * self.kv_heads


def kernel(
    plan,
    res_ref, attn_ref, ffn_ref, len_ref, pos_ref,
    query_hbm, keyval_hbm, output_hbm, keys_hbm, values_hbm, gate_hbm, up_hbm, down_hbm,
    out_ref,
    query_buf, keyval_buf, output_buf, keys_buf, values_buf, ffn_buf, extra_buf,
    normed_ref, pack_ref, spread_ref, kv_ref, new_key_ref, new_value_ref,
    send1, recv1, rot, pay, recv_pay, att, out_lhs, wide_acc,
    part_send, part_recv, normed2_ref, hidden_ref, square_ref,
    ffn_pack, ffn_send, ffn_recv, act, down_lhs, last_send, last_recv,
    query_sem, keyval_sem, cache_sem, output_sem, ffn_sem, down_sem,
    s1, r1, s2, r2, s3, r3, s4, r4, s5, r5, s6, r6, s7, r7, s8, r8,
):
    n, wides, shorts, subs = plan.members, plan.wide, plan.short, plan.sub
    answers, groups = plan.answers, plan.groups
    wide, short, sub = lax.axis_index("wide"), lax.axis_index("short"), lax.axis_index("sub")
    me = wide * subs + sub
    all_own = plan.owners == n

    def member(rank):
        return {"wide": rank // subs, "sub": rank % subs}

    def owned(rank, body):
        if all_own:
            body()
        else:
            pl.when(rank < plan.owners)(body)

    def remote(src, dst, ssem, rsem, device):
        return pltpu.make_async_remote_copy(
            src_ref=src, dst_ref=dst, send_sem=ssem, recv_sem=rsem,
            device_id=device, device_id_type=pl.DeviceIdType.MESH,
        )

    barrier = pltpu.get_barrier_semaphore()
    for o in range(1, n):
        pl.semaphore_signal(
            barrier, inc=1, device_id=member(lax.rem(me + o, n)),
            device_id_type=pl.DeviceIdType.MESH,
        )
    for o in range(1, shorts):
        pl.semaphore_signal(
            barrier, inc=1, device_id={"short": lax.rem(short + o, shorts)},
            device_id_type=pl.DeviceIdType.MESH,
        )

    q_rows = plan.width // plan.query_chunks
    o_rows = plan.out_rows // plan.out_chunks

    def query_copy(c):
        at = pl.ds(c * q_rows, q_rows)
        return pltpu.make_async_copy(query_hbm.at[at], query_buf.at[at], query_sem.at[c])

    def output_copy(c):
        at = pl.ds(c * o_rows, o_rows)
        return pltpu.make_async_copy(output_hbm.at[at], output_buf.at[at], output_sem.at[c])

    keyval_copy = pltpu.make_async_copy(keyval_hbm, keyval_buf, keyval_sem.at[0])
    keys_copy = pltpu.make_async_copy(keys_hbm, keys_buf, cache_sem.at[0])
    values_copy = pltpu.make_async_copy(values_hbm, values_buf, cache_sem.at[1])

    def ffn_rank(i):
        return lax.rem(me + 1 + i, n)

    def ffn_copies(i):
        slot = lax.rem(i, plan.slots)
        at = pl.ds(pl.multiple_of(ffn_rank(i) * plan.piece, lane), plan.piece)
        return [
            pltpu.make_async_copy(
                hbm.at[:, at],
                ffn_buf.at[slot, :, pl.ds(k * plan.piece, plan.piece)],
                ffn_sem.at[slot, k],
            )
            for k, hbm in enumerate((gate_hbm, up_hbm))
        ]

    def ffn_start(i):
        def body():
            for copy in ffn_copies(i):
                copy.start()

        owned(ffn_rank(i), body)

    def down_rank(j):
        return lax.rem(me - j + n, n)

    def down_place(j):
        kind, k = plan.places[j]
        if kind == "slot":
            at = (n - plan.slots + k) % plan.slots
            return ffn_buf.at[at, pl.ds(0, plan.piece), pl.ds(0, plan.out_cols)]
        buf = {"query": query_buf, "out": output_buf, "extra": extra_buf}[kind]
        return buf.at[pl.ds(k * plan.piece, plan.piece), pl.ds(0, plan.out_cols)]

    def down_copy(j):
        at = pl.ds(pl.multiple_of(down_rank(j) * plan.piece, lane), plan.piece)
        return pltpu.make_async_copy(down_hbm.at[at], down_place(j), down_sem.at[j])

    def down_start(j):
        owned(down_rank(j), lambda: down_copy(j).start())

    keyval_copy.start()
    for c in range(plan.query_chunks):
        query_copy(c).start()
    keys_copy.start()
    values_copy.start()
    queue = [functools.partial(lambda c: output_copy(c).start(), c) for c in range(plan.out_chunks)]
    queue += [functools.partial(ffn_start, i) for i in range(plan.slots)]

    resid = res_ref[...].astype(f32)
    normed_ref[...] = (resid * attn_ref[...].astype(f32)).astype(bf16)
    squares = jnp.sum(resid * resid, axis=1, keepdims=True)

    row16 = lax.broadcasted_iota(jnp.int32, (16, lane), 0)
    lane16 = lax.broadcasted_iota(jnp.int32, (16, lane), 1)
    group16 = row16 // answers
    answer16 = row16 % answers
    position = jnp.zeros((16, lane), f32)
    for a in range(answers):
        position = jnp.where(answer16 == a, pos_ref[a].astype(f32), position)
    freq = jnp.exp((lane16 % (lane // 2)).astype(f32) * (-2.0 / lane * math.log(rope_base)))
    angle = position * freq
    cosine = jnp.cos(angle)
    sine = jnp.sin(angle)
    sine = jnp.where(lane16 < lane // 2, -sine, sine)
    ffn_pack[...] = jnp.zeros_like(ffn_pack)

    keyval_copy.wait()
    kv_part = jnp.dot(normed_ref[...], keyval_buf[...], preferred_element_type=f32)
    q_part = jnp.zeros((answers, plan.query_cols), f32)
    share = -(-len(queue) // plan.query_chunks)
    for c in range(plan.query_chunks):
        query_copy(c).wait()
        for _ in range(share):
            if queue:
                queue.pop(0)()
        at = pl.ds(c * q_rows, q_rows)
        q_part += jnp.dot(normed_ref[:, at], query_buf[at, :], preferred_element_type=f32)
    for j, (kind, _) in enumerate(plan.places):
        if kind in ("query", "extra"):
            down_start(j)

    def place(k):
        g, first = k % groups, k // groups * lane
        return slice(g * answers, (g + 1) * answers), slice(first, first + lane)

    def tiles_of(value):
        return [value[:, k * lane : (k + 1) * lane] for k in range(value.shape[1] // lane)]

    packed = tiles_of(q_part) + tiles_of(kv_part)
    packed += split_two(jnp.broadcast_to(squares, (answers, lane)))
    pack_ref[...] = jnp.zeros_like(pack_ref)
    for k, tile in enumerate(packed):
        pack_ref[place(k)] = tile
    send1[...] = pack_ref[...].astype(bf16)

    pl.semaphore_wait(barrier, n - 1 + shorts - 1)

    def copy1(o):
        return remote(
            send1, recv1.at[o - 1], s1.at[o - 1], r1.at[o - 1],
            {"wide": lax.rem(wide + o, wides)},
        )

    for o in range(1, wides):
        copy1(o).start()
    for o in range(1, wides):
        copy1(o).wait_recv()
        pack_ref[...] += recv1[o - 1].astype(f32)

    def spread(four):
        for g in range(groups):
            spread_ref[g * answers : (g + 1) * answers, :] = four
        return spread_ref[...]

    square_at = plan.heads + plan.blocks
    total = pack_ref[place(square_at)] + pack_ref[place(square_at + 1)]
    factor = spread(lax.rsqrt(total / plan.model + epsilon))
    for t in range(plan.pack_cols // lane):
        value = pack_ref[:, t * lane : (t + 1) * lane] * factor
        turned = value * cosine + pltpu.roll(value, lane // 2, 1) * sine
        if (t + 1) * groups > plan.heads:
            block = t * groups + group16 - plan.heads
            is_value = (block >= 0) & ((sub * plan.blocks + block + 2) % 2 == 1)
            turned = jnp.where(is_value, value, turned)
        rot[sub, :, t * lane : (t + 1) * lane] = turned.astype(bf16)

    def copy2(o, source):
        return remote(
            rot.at[source], rot.at[source], s2.at[o - 1], r2.at[o - 1],
            {"sub": lax.rem(sub + o, subs)},
        )

    for o in range(1, subs):
        copy2(o, sub).start()
    for o in range(1, subs):
        copy2(o, lax.rem(sub - o + subs, subs)).wait_recv()

    keys_copy.wait()
    values_copy.wait()
    scaling = 1.0 / math.sqrt(lane)
    heads = plan.head_tiles
    sharers = subs // plan.kv_heads
    stacked = sharers * heads * 16
    row_id = lax.broadcasted_iota(jnp.int32, (stacked, plan.rows), 0)
    col_id = lax.broadcasted_iota(jnp.int32, (stacked, plan.rows), 1) + me * plan.rows
    valid = [(row_id % answers == a) & (col_id < len_ref[a]) for a in range(answers)]

    def copy3(u, source):
        return remote(pay.at[u], recv_pay.at[source], s3.at[u], r3.at[source], member(u))

    for h in range(plan.kv_heads):
        queries = jnp.concatenate(
            [
                rot[s, :, t * lane : (t + 1) * lane]
                for s in range(h * sharers, (h + 1) * sharers)
                for t in range(heads)
            ],
            axis=0,
        )
        for k, new_ref in enumerate((new_key_ref, new_value_ref)):
            block = 2 * h + k
            rows, columns = place(plan.heads + block % plan.blocks)
            kv_ref[...] = rot[block // plan.blocks, :, columns].astype(f32)
            for g in range(groups):
                new_ref[g * answers : (g + 1) * answers, :] = kv_ref[rows, :]
        new_key = jnp.concatenate([new_key_ref[...]] * (sharers * heads), axis=0)
        new_value = jnp.concatenate([new_value_ref[...]] * (sharers * heads), axis=0)
        own = jnp.sum(queries.astype(f32) * new_key, axis=1, keepdims=True) * scaling
        scores = []
        for a in range(answers):
            score = lax.dot_general(
                queries, keys_buf[a, h], (((1,), (1,)), ((), ())), preferred_element_type=f32
            )
            scores.append(jnp.where(valid[a], score * scaling, neg_large))
        top = functools.reduce(jnp.maximum, scores)
        top = jnp.max(top, axis=1, keepdims=True)
        top = jnp.where(me == 0, jnp.maximum(top, own), top)
        own_weight = jnp.where(me == 0, jnp.exp(own - top), 0.0)
        totals = own_weight
        mixed = own_weight * new_value
        for a in range(answers):
            weights = jnp.where(valid[a], jnp.exp(scores[a] - top), 0.0).astype(bf16)
            totals += jnp.sum(weights.astype(f32), axis=1, keepdims=True)
            mixed += jnp.dot(weights, values_buf[a, h], preferred_element_type=f32)
        for t in range(sharers * heads):
            u = h * sharers * heads + t
            rows = slice(t * 16, (t + 1) * 16)
            top_high, rest = split_two(jnp.broadcast_to(top[rows], (16, lane)))
            top_mid, top_low = split_two(rest)
            sum_high, sum_low = split_two(jnp.broadcast_to(totals[rows], (16, lane)))
            stats = jnp.where(lane16 < 64, sum_high, sum_low)
            stats = jnp.where(lane16 < 48, top_low, stats)
            stats = jnp.where(lane16 < 32, top_mid, stats)
            stats = jnp.where(lane16 < 16, top_high, stats)
            pay[u, :16, :] = mixed[rows].astype(bf16)
            pay[u, 16:, :] = stats.astype(bf16)

            @pl.when(me != u)
            def _():
                copy3(u, me).start()

    def copy4(o, source):
        return remote(
            att.at[source], att.at[source], s4.at[o - 1], r4.at[source],
            member(lax.rem(me + o, n)),
        )

    @pl.when(me < plan.units)
    def _():
        parts = [pay[me].astype(f32)]
        for o in range(1, n):
            source = lax.rem(me + o, n)
            copy3(0, source).wait_recv()
            parts.append(recv_pay[source].astype(f32))
        tops = [
            p[16:, 0:1] + p[16:, 16:17] + p[16:, 32:33] for p in parts
        ]
        highest = functools.reduce(jnp.maximum, tops)
        numerator = jnp.zeros((16, lane), f32)
        denominator = jnp.zeros((16, 1), f32)
        for p, top in zip(parts, tops):
            scale = jnp.exp(top - highest)
            numerator += p[:16] * scale
            denominator += (p[16:, 48:49] + p[16:, 64:65]) * scale
        att[me] = (numerator / denominator).astype(bf16)
        for o in range(1, n):
            copy4(o, me).start()

    for u in range(plan.units):

        @pl.when(me != u)
        def _():
            copy4(1, u).wait_recv()

    for u in range(plan.units):
        block = att[u].astype(f32)
        for g in range(groups):
            head = (u % heads) * groups + g
            if head >= plan.heads:
                continue
            head += u // heads * plan.heads
            out_lhs[:, head * lane : (head + 1) * lane] = jnp.where(
                group16 == g, block, 0.0
            ).astype(bf16)
    product = jnp.zeros((16, plan.out_cols), f32)
    for c in range(plan.out_chunks):
        output_copy(c).wait()
        at = pl.ds(c * o_rows, o_rows)
        product += jnp.dot(out_lhs[:, at], output_buf[at, :], preferred_element_type=f32)
    for j, (kind, _) in enumerate(plan.places):
        if kind == "out":
            down_start(j)

    def folded(value):
        wide_acc[...] = value
        return functools.reduce(
            jnp.add, [wide_acc[g * answers : (g + 1) * answers, :] for g in range(groups)]
        )

    def across_short(value, send, recv, ssem, rsem):
        send[...] = value
        copies = [
            remote(
                send, recv.at[o - 1], ssem.at[o - 1], rsem.at[o - 1],
                {"short": lax.rem(short + o, shorts)},
            )
            for o in range(1, shorts)
        ]
        for copy in copies:
            copy.start()
        for o, copy in enumerate(copies):
            copy.wait_recv()
            value += recv[o]
        return value

    resid_part = res_ref[:, : plan.out_cols].astype(f32)
    for k in range(1, subs):
        here = res_ref[:, k * plan.out_cols : (k + 1) * plan.out_cols].astype(f32)
        resid_part = jnp.where(sub == k, here, resid_part)
    hidden = resid_part + across_short(folded(product), part_send, part_recv, s5, r5)
    hidden_ref[...] = hidden
    normed2_ref[...] = (hidden * ffn_ref[...].astype(f32)).astype(bf16)
    high, low = split_two(
        jnp.broadcast_to(jnp.sum(hidden * hidden, axis=1, keepdims=True), (answers, lane))
    )
    square_ref[0] = high
    square_ref[1] = low

    def ffn_place(t, k):
        rows, columns = place(t)
        first = columns.start + k * plan.half
        return rows, slice(first, first + lane)

    def ffn_piece(i):
        slot = lax.rem(i, plan.slots)
        for copy in ffn_copies(i):
            copy.wait()
        for k in range(2):
            part = jnp.dot(
                normed2_ref[...],
                ffn_buf[slot, :, pl.ds(k * plan.piece, plan.piece)],
                preferred_element_type=f32,
            )
            for t, tile in enumerate(tiles_of(part) + [square_ref[k]]):
                ffn_pack[ffn_place(t, k)] = tile

    def copy6(i):
        return remote(
            ffn_send.at[i], ffn_recv.at[i], s6.at[i], r6.at[i], member(ffn_rank(i))
        )

    def ffn_freed(i):
        @pl.when(i + plan.slots < n)
        def _():
            ffn_start(i + plan.slots)

        for j, (kind, k) in enumerate(plan.places):
            if kind == "slot":

                @pl.when(i == n - plan.slots + k)
                def _():
                    down_start(j)

    def ffn_step(i, carry):
        def body():
            ffn_piece(i)
            ffn_send[i] = ffn_pack[...].astype(bf16)
            copy6(i).start()

        owned(ffn_rank(i), body)
        ffn_freed(i)
        return carry

    lax.fori_loop(0, n - 1, ffn_step, 0)

    def copy7(o):
        return remote(
            act.at[n - 1], act.at[o - 1], s7.at[o - 1], r7.at[o - 1],
            member(lax.rem(me + o, n)),
        )

    def activate():
        ffn_piece(n - 1)
        for i in range(n - 1):
            copy6(i).wait_recv()
            ffn_pack[...] += ffn_recv[i].astype(f32)
        total2 = ffn_pack[ffn_place(plan.tiles, 0)] + ffn_pack[ffn_place(plan.tiles, 1)]
        factor2 = spread(lax.rsqrt(total2 / plan.model + epsilon))
        for t in range(plan.half // lane):
            gate = ffn_pack[:, t * lane : (t + 1) * lane] * factor2
            upward = ffn_pack[:, plan.half + t * lane : plan.half + (t + 1) * lane] * factor2
            act[n - 1, :, t * lane : (t + 1) * lane] = (
                gate / (1.0 + jnp.exp(-gate)) * upward
            ).astype(bf16)
        for o in range(1, n):
            copy7(o).start()

    owned(me, activate)
    ffn_freed(n - 1)

    wide_acc[...] = jnp.zeros_like(wide_acc)
    for j in range(n):

        def down_piece():
            if j:
                copy7(j).wait_recv()
            down_copy(j).wait()
            block = act[(j - 1) % n].astype(f32)
            for k in range(plan.tiles):
                first = (k // groups) * lane
                down_lhs[:, k * lane : (k + 1) * lane] = jnp.where(
                    group16 == k % groups, block[:, first : first + lane], 0.0
                ).astype(bf16)
            wide_acc[...] += jnp.dot(
                down_lhs[...], down_place(j)[...], preferred_element_type=f32
            )

        owned(down_rank(j), down_piece)
    projected = across_short(folded(wide_acc[...]), last_send, last_recv, s8, r8)
    out_ref[...] = (hidden_ref[...] + projected).astype(bf16)

    for o in range(1, wides):
        copy1(o).wait_send()
    for o in range(1, subs):
        copy2(o, sub).wait_send()
    for u in range(plan.units):

        @pl.when(me != u)
        def _():
            copy3(u, me).wait_send()

    @pl.when(me < plan.units)
    def _():
        for o in range(1, n):
            copy4(o, me).wait_send()

    for o in range(1, shorts):
        for send, recv, ssem, rsem in (
            (part_send, part_recv, s5, r5), (last_send, last_recv, s8, r8)
        ):
            remote(
                send, recv.at[o - 1], ssem.at[o - 1], rsem.at[o - 1],
                {"short": lax.rem(short + o, shorts)},
            ).wait_send()
    for i in range(n - 1):
        owned(ffn_rank(i), lambda: copy6(i).wait_send())

    def sent7():
        for o in range(1, n):
            copy7(o).wait_send()

    owned(me, sent7)


def per_device(
    sizes, residual, attn_gain, query_weight, key_value_weight, output_weight, cache_keys,
    cached_value_rows, lengths, positions, ffn_gain, gate_weight, up_weight, down_weight,
):
    plan = Plan(
        sizes, residual.shape, query_weight.shape, key_value_weight.shape, output_weight.shape,
        cache_keys.shape, gate_weight.shape, down_weight.shape,
    )
    n, answers = plan.members, plan.answers
    vmem = pl.BlockSpec(memory_space=pltpu.VMEM)
    smem = pl.BlockSpec(memory_space=pltpu.SMEM)
    hbm = pl.BlockSpec(memory_space=pltpu.HBM)
    dma = pltpu.SemaphoreType.DMA
    short_peers = max(plan.short - 1, 1)
    scratch = [
        pltpu.VMEM(query_weight.shape, bf16),
        pltpu.VMEM(key_value_weight.shape, bf16),
        pltpu.VMEM(output_weight.shape, bf16),
        pltpu.VMEM(cache_keys.shape, bf16),
        pltpu.VMEM(cache_keys.shape, bf16),
        pltpu.VMEM((plan.slots, plan.gate_rows, 2 * plan.piece), bf16),
        pltpu.VMEM((plan.extra, plan.out_cols), bf16),
        pltpu.VMEM((answers, plan.width), bf16),
        pltpu.VMEM((16, plan.pack_cols), f32),
        pltpu.VMEM((16, lane), f32),
        pltpu.VMEM((16, lane), f32),
        pltpu.VMEM((16, lane), f32),
        pltpu.VMEM((16, lane), f32),
        pltpu.VMEM((16, plan.pack_cols), bf16),
        pltpu.VMEM((plan.wide - 1, 16, plan.pack_cols), bf16),
        pltpu.VMEM((plan.sub, 16, plan.pack_cols), bf16),
        pltpu.VMEM((plan.units, 32, lane), bf16),
        pltpu.VMEM((n, 32, lane), bf16),
        pltpu.VMEM((plan.units, 16, lane), bf16),
        pltpu.VMEM((16, plan.out_rows), bf16),
        pltpu.VMEM((16, plan.out_cols), f32),
        pltpu.VMEM((answers, plan.out_cols), f32),
        pltpu.VMEM((short_peers, answers, plan.out_cols), f32),
        pltpu.VMEM((answers, plan.out_cols), bf16),
        pltpu.VMEM((answers, plan.out_cols), f32),
        pltpu.VMEM((2, answers, lane), f32),
        pltpu.VMEM((16, 2 * plan.half), f32),
        pltpu.VMEM((n - 1, 16, 2 * plan.half), bf16),
        pltpu.VMEM((n - 1, 16, 2 * plan.half), bf16),
        pltpu.VMEM((n, 16, plan.half), bf16),
        pltpu.VMEM((16, plan.piece), bf16),
        pltpu.VMEM((answers, plan.out_cols), f32),
        pltpu.VMEM((short_peers, answers, plan.out_cols), f32),
        dma((plan.query_chunks,)),
        dma((1,)),
        dma((2,)),
        dma((plan.out_chunks,)),
        dma((plan.slots, 2)),
        dma((n,)),
        dma((plan.wide - 1,)), dma((plan.wide - 1,)),
        dma((plan.sub - 1,)), dma((plan.sub - 1,)),
        dma((plan.units,)), dma((n,)),
        dma((n - 1,)), dma((plan.units,)),
        dma((short_peers,)), dma((short_peers,)),
        dma((n - 1,)), dma((n - 1,)),
        dma((n - 1,)), dma((n - 1,)),
        dma((short_peers,)), dma((short_peers,)),
    ]
    return pl.pallas_call(
        functools.partial(kernel, plan),
        out_shape=jax.ShapeDtypeStruct((answers, plan.out_cols), bf16),
        in_specs=[vmem, vmem, vmem, smem, smem] + [hbm] * 8,
        out_specs=vmem,
        scratch_shapes=scratch,
        compiler_params=pltpu.CompilerParams(
            collective_id=0, has_side_effects=True, vmem_limit_bytes=vmem_limit
        ),
        name="layer",
    )(
        residual, attn_gain.reshape(1, -1), ffn_gain.reshape(1, -1), lengths, positions,
        query_weight, key_value_weight, output_weight, cache_keys, cached_value_rows,
        gate_weight, up_weight, down_weight,
    )


def solution(mesh):
    sizes = (mesh.shape["wide"], mesh.shape["short"], mesh.shape["sub"])
    placed = (
        P("groups", "wide"),
        P("wide"),
        P("wide", ("short", "sub")),
        P("wide", ("short", "sub")),
        P("short", ("wide", "sub")),
        P("groups", "short", ("wide", "sub"), None),
        P("groups", "short", ("wide", "sub"), None),
        P("groups"),
        P("groups"),
        P(("wide", "sub")),
        P(("wide", "sub"), "short"),
        P(("wide", "sub"), "short"),
        P("short", ("wide", "sub")),
    )
    return jax.shard_map(
        functools.partial(per_device, sizes),
        mesh=mesh,
        in_specs=placed,
        out_specs=P("groups", ("wide", "sub")),
        check_vma=False,
    )
```

```python
import functools
import math

import jax
import jax.numpy as jnp
from jax import lax
from jax.experimental import pallas as pl
from jax.experimental.pallas import tpu as pltpu
from jax.sharding import PartitionSpec as P

rope_base = 1000000.0
epsilon = 1e-05
neg_large = -1e30
lane = 128
bf16 = jnp.bfloat16
f32 = jnp.float32
vmem_limit = 63 * 2**20
lag = 2


def split_two(value):
    high = value.astype(bf16).astype(f32)
    return high, value - high


def largest_divisor(count, most):
    return max(d for d in range(1, most + 1) if count % d == 0)


class Plan:
    def __init__(self, sizes, residual, query, keyval, output, cache, gate, down):
        self.wide, self.short, self.sub, self.pair = sizes
        self.members = self.wide * self.sub
        self.answers, self.width = residual
        self.groups = 16 // self.answers
        self.model = self.width * self.wide
        self.query_cols = query[1]
        self.heads = self.query_cols // lane
        self.blocks = keyval[1] // lane
        self.head_tiles = -(-self.heads // self.groups)
        self.pack_cols = -(-(self.heads + self.blocks + 2) // self.groups) * lane
        self.kv_heads = cache[1]
        self.rows = cache[2]
        self.units = self.sub * self.head_tiles
        self.out_rows, self.out_cols = output
        self.gate_rows, whole_ff = gate
        self.ff = whole_ff // self.pair
        self.all_answers = self.answers * self.pair
        self.folds = 16 // self.all_answers
        self.planes = self.pair * self.short
        self.owners = largest_divisor(self.ff // lane, self.members)
        self.piece = self.ff // self.owners
        self.tiles = self.piece // lane
        self.half = -(-(self.tiles + 1) // self.folds) * lane
        self.query_chunks = largest_divisor(self.width // lane, 6)
        self.out_chunks = largest_divisor(self.out_rows // lane, 6)
        assert self.all_answers * self.folds == 16 and self.ff * self.pair == whole_ff
        assert self.units <= self.members and self.sub % self.kv_heads == 0
        assert self.blocks * self.sub == 2 * self.kv_heads


def kernel(
    plan,
    res_ref, attn_ref, ffn_ref, len_ref, pos_ref,
    query_hbm, keyval_hbm, output_hbm, keys_hbm, values_hbm, gate_hbm, up_hbm, down_hbm,
    out_ref,
    query_buf, keyval_buf, output_buf, keys_buf, values_buf, ffn_buf, down_buf,
    normed_ref, pack_ref, spread_ref, kv_ref, new_key_ref, new_value_ref,
    send1, recv1, rot, pay, recv_pay, att, out_lhs, wide_acc,
    part_all, normed2_ref, hidden_ref, both_ref, square_ref,
    ffn_pack, ffn_sum, ffn_send, ffn_recv, act, down_lhs, last_part, last_recv,
    query_sem, keyval_sem, cache_sem, output_sem, ffn_sem, down_sem,
    s1, r1, s2, r2, s3, r3, s4, r4, s5, r5, s6, r6, s7, r7, s8, r8,
):
    n, wides, shorts, subs = plan.members, plan.wide, plan.short, plan.sub
    answers, groups = plan.answers, plan.groups
    wide, short, sub = lax.axis_index("wide"), lax.axis_index("short"), lax.axis_index("sub")
    part = lax.axis_index("groups")
    planes = plan.planes
    plane = part * shorts + short
    me = wide * subs + sub
    owners = plan.owners

    def member(rank):
        return {"wide": rank // subs, "sub": rank % subs}

    def remote(src, dst, ssem, rsem, device):
        return pltpu.make_async_remote_copy(
            src_ref=src, dst_ref=dst, send_sem=ssem, recv_sem=rsem,
            device_id=device, device_id_type=pl.DeviceIdType.MESH,
        )

    barrier = pltpu.get_barrier_semaphore()
    for o in range(1, n):
        pl.semaphore_signal(
            barrier, inc=1, device_id=member(lax.rem(me + o, n)),
            device_id_type=pl.DeviceIdType.MESH,
        )
    def in_plane(rank):
        return {"groups": rank // shorts, "short": rank % shorts}

    for o in range(1, planes):
        pl.semaphore_signal(
            barrier, inc=1, device_id=in_plane(lax.rem(plane + o, planes)),
            device_id_type=pl.DeviceIdType.MESH,
        )

    q_rows = plan.width // plan.query_chunks
    o_rows = plan.out_rows // plan.out_chunks

    def query_copy(c):
        at = pl.ds(c * q_rows, q_rows)
        return pltpu.make_async_copy(query_hbm.at[at], query_buf.at[at], query_sem.at[c])

    def output_copy(c):
        at = pl.ds(c * o_rows, o_rows)
        return pltpu.make_async_copy(output_hbm.at[at], output_buf.at[at], output_sem.at[c])

    keyval_copy = pltpu.make_async_copy(keyval_hbm, keyval_buf, keyval_sem.at[0])
    keys_copy = pltpu.make_async_copy(keys_hbm, keys_buf, cache_sem.at[0])
    values_copy = pltpu.make_async_copy(values_hbm, values_buf, cache_sem.at[1])

    def ffn_copies(i):
        at = pl.ds(pl.multiple_of(part * plan.ff + i * plan.piece, lane), plan.piece)
        return [
            pltpu.make_async_copy(
                hbm.at[:, at],
                ffn_buf.at[i, :, pl.ds(k * plan.piece, plan.piece)],
                ffn_sem.at[i, k],
            )
            for k, hbm in enumerate((gate_hbm, up_hbm))
        ]

    def ffn_start(i):
        for copy in ffn_copies(i):
            copy.start()

    def down_copy(j):
        at = pl.ds(pl.multiple_of(part * plan.ff + j * plan.piece, lane), plan.piece)
        here = pl.ds(pl.multiple_of(j * plan.piece, lane), plan.piece)
        return pltpu.make_async_copy(down_hbm.at[at], down_buf.at[here], down_sem.at[j])

    keyval_copy.start()
    for c in range(plan.query_chunks):
        query_copy(c).start()
    keys_copy.start()
    values_copy.start()
    begun = [0]

    def ffn_begin(sevenths):
        upto = -(-owners * sevenths // 7)
        for i in range(begun[0], upto):
            ffn_start(i)
        begun[0] = upto

    resid = res_ref[...].astype(f32)
    normed_ref[...] = (resid * attn_ref[...].astype(f32)).astype(bf16)
    squares = jnp.sum(resid * resid, axis=1, keepdims=True)

    row16 = lax.broadcasted_iota(jnp.int32, (16, lane), 0)
    lane16 = lax.broadcasted_iota(jnp.int32, (16, lane), 1)
    group16 = row16 // answers
    answer16 = row16 % answers
    position = jnp.zeros((16, lane), f32)
    for a in range(answers):
        position = jnp.where(answer16 == a, pos_ref[a].astype(f32), position)
    freq = jnp.exp((lane16 % (lane // 2)).astype(f32) * (-2.0 / lane * math.log(rope_base)))
    angle = position * freq
    cosine = jnp.cos(angle)
    sine = jnp.sin(angle)
    sine = jnp.where(lane16 < lane // 2, -sine, sine)
    ffn_pack[...] = jnp.zeros_like(ffn_pack)

    keyval_copy.wait()
    kv_part = jnp.dot(normed_ref[...], keyval_buf[...], preferred_element_type=f32)
    q_part = jnp.zeros((answers, plan.query_cols), f32)
    for c in range(plan.query_chunks):
        query_copy(c).wait()
        at = pl.ds(c * q_rows, q_rows)
        q_part += jnp.dot(normed_ref[:, at], query_buf[at, :], preferred_element_type=f32)
    def place(k):
        g, first = k % groups, k // groups * lane
        return slice(g * answers, (g + 1) * answers), slice(first, first + lane)

    def tiles_of(value):
        return [value[:, k * lane : (k + 1) * lane] for k in range(value.shape[1] // lane)]

    packed = tiles_of(q_part) + tiles_of(kv_part)
    packed += split_two(jnp.broadcast_to(squares, (answers, lane)))
    pack_ref[...] = jnp.zeros_like(pack_ref)
    for k, tile in enumerate(packed):
        pack_ref[place(k)] = tile
    send1[...] = pack_ref[...].astype(bf16)

    pl.semaphore_wait(barrier, n - 1 + planes - 1)

    def copy1(o):
        return remote(
            send1, recv1.at[o - 1], s1.at[o - 1], r1.at[o - 1],
            {"wide": lax.rem(wide + o, wides)},
        )

    for o in range(1, wides):
        copy1(o).start()
    for c in range(plan.out_chunks):
        output_copy(c).start()
    for o in range(1, wides):
        copy1(o).wait_recv()
        pack_ref[...] += recv1[o - 1].astype(f32)

    def spread(four):
        for g in range(groups):
            spread_ref[g * answers : (g + 1) * answers, :] = four
        return spread_ref[...]

    square_at = plan.heads + plan.blocks
    total = pack_ref[place(square_at)] + pack_ref[place(square_at + 1)]
    factor = spread(lax.rsqrt(total / plan.model + epsilon))
    for t in range(plan.pack_cols // lane):
        value = pack_ref[:, t * lane : (t + 1) * lane] * factor
        turned = value * cosine + pltpu.roll(value, lane // 2, 1) * sine
        if (t + 1) * groups > plan.heads:
            block = t * groups + group16 - plan.heads
            is_value = (block >= 0) & ((sub * plan.blocks + block + 2) % 2 == 1)
            turned = jnp.where(is_value, value, turned)
        rot[sub, :, t * lane : (t + 1) * lane] = turned.astype(bf16)

    def copy2(o, source):
        return remote(
            rot.at[source], rot.at[source], s2.at[o - 1], r2.at[o - 1],
            {"sub": lax.rem(sub + o, subs)},
        )

    for o in range(1, subs):
        copy2(o, sub).start()
    ffn_begin(1)
    for o in range(1, subs):
        copy2(o, lax.rem(sub - o + subs, subs)).wait_recv()

    keys_copy.wait()
    values_copy.wait()
    scaling = 1.0 / math.sqrt(lane)
    heads = plan.head_tiles
    sharers = subs // plan.kv_heads
    stacked = sharers * heads * 16
    row_id = lax.broadcasted_iota(jnp.int32, (stacked, plan.rows), 0)
    col_id = lax.broadcasted_iota(jnp.int32, (stacked, plan.rows), 1) + me * plan.rows
    valid = [(row_id % answers == a) & (col_id < len_ref[a]) for a in range(answers)]

    def copy3(u, source):
        return remote(pay.at[u], recv_pay.at[source], s3.at[u], r3.at[source], member(u))

    for h in range(plan.kv_heads):
        queries = jnp.concatenate(
            [
                rot[s, :, t * lane : (t + 1) * lane]
                for s in range(h * sharers, (h + 1) * sharers)
                for t in range(heads)
            ],
            axis=0,
        )
        for k, new_ref in enumerate((new_key_ref, new_value_ref)):
            block = 2 * h + k
            rows, columns = place(plan.heads + block % plan.blocks)
            kv_ref[...] = rot[block // plan.blocks, :, columns].astype(f32)
            for g in range(groups):
                new_ref[g * answers : (g + 1) * answers, :] = kv_ref[rows, :]
        new_key = jnp.concatenate([new_key_ref[...]] * (sharers * heads), axis=0)
        new_value = jnp.concatenate([new_value_ref[...]] * (sharers * heads), axis=0)
        own = jnp.sum(queries.astype(f32) * new_key, axis=1, keepdims=True) * scaling
        scores = []
        for a in range(answers):
            score = lax.dot_general(
                queries, keys_buf[a, h], (((1,), (1,)), ((), ())), preferred_element_type=f32
            )
            scores.append(jnp.where(valid[a], score * scaling, neg_large))
        top = functools.reduce(jnp.maximum, scores)
        top = jnp.max(top, axis=1, keepdims=True)
        top = jnp.where(me == 0, jnp.maximum(top, own), top)
        own_weight = jnp.where(me == 0, jnp.exp(own - top), 0.0)
        totals = own_weight
        mixed = own_weight * new_value
        for a in range(answers):
            weights = jnp.where(valid[a], jnp.exp(scores[a] - top), 0.0).astype(bf16)
            totals += jnp.sum(weights.astype(f32), axis=1, keepdims=True)
            mixed += jnp.dot(weights, values_buf[a, h], preferred_element_type=f32)
        for t in range(sharers * heads):
            u = h * sharers * heads + t
            rows = slice(t * 16, (t + 1) * 16)
            top_high, rest = split_two(jnp.broadcast_to(top[rows], (16, lane)))
            top_mid, top_low = split_two(rest)
            sum_high, sum_low = split_two(jnp.broadcast_to(totals[rows], (16, lane)))
            stats = jnp.where(lane16 < 64, sum_high, sum_low)
            stats = jnp.where(lane16 < 48, top_low, stats)
            stats = jnp.where(lane16 < 32, top_mid, stats)
            stats = jnp.where(lane16 < 16, top_high, stats)
            pay[u, :16, :] = mixed[rows].astype(bf16)
            pay[u, 16:, :] = stats.astype(bf16)

            @pl.when(me != u)
            def _():
                copy3(u, me).start()

    ffn_begin(3)

    def copy4(o, source):
        return remote(
            att.at[source], att.at[source], s4.at[o - 1], r4.at[source],
            member(lax.rem(me + o, n)),
        )

    @pl.when(me < plan.units)
    def _():
        parts = [pay[me].astype(f32)]
        for o in range(1, n):
            source = lax.rem(me + o, n)
            copy3(0, source).wait_recv()
            parts.append(recv_pay[source].astype(f32))
        tops = [
            p[16:, 0:1] + p[16:, 16:17] + p[16:, 32:33] for p in parts
        ]
        highest = functools.reduce(jnp.maximum, tops)
        numerator = jnp.zeros((16, lane), f32)
        denominator = jnp.zeros((16, 1), f32)
        for p, top in zip(parts, tops):
            scale = jnp.exp(top - highest)
            numerator += p[:16] * scale
            denominator += (p[16:, 48:49] + p[16:, 64:65]) * scale
        att[me] = (numerator / denominator).astype(bf16)
        for o in range(1, n):
            copy4(o, me).start()

    ffn_begin(5)
    for u in range(plan.units):

        @pl.when(me != u)
        def _():
            copy4(1, u).wait_recv()

    for u in range(plan.units):
        block = att[u].astype(f32)
        for g in range(groups):
            head = (u % heads) * groups + g
            if head >= plan.heads:
                continue
            head += u // heads * plan.heads
            out_lhs[:, head * lane : (head + 1) * lane] = jnp.where(
                group16 == g, block, 0.0
            ).astype(bf16)
    product = jnp.zeros((16, plan.out_cols), f32)
    for c in range(plan.out_chunks):
        output_copy(c).wait()
        at = pl.ds(c * o_rows, o_rows)
        product += jnp.dot(out_lhs[:, at], output_buf[at, :], preferred_element_type=f32)
    def folded(value, rows):
        wide_acc[...] = value
        return functools.reduce(
            jnp.add, [wide_acc[r : r + rows, :] for r in range(0, 16, rows)]
        )

    resid_part = res_ref[:, : plan.out_cols].astype(f32)
    for k in range(1, subs):
        here = res_ref[:, k * plan.out_cols : (k + 1) * plan.out_cols].astype(f32)
        resid_part = jnp.where(sub == k, here, resid_part)
    part_all[plane] = folded(product, answers) + jnp.where(short == 0, resid_part, 0.0)

    def copy5(o, source):
        return remote(
            part_all.at[source], part_all.at[source], s5.at[o - 1], r5.at[source],
            in_plane(lax.rem(plane + o, planes)),
        )

    for o in range(1, planes):
        copy5(o, plane).start()
    ffn_begin(7)
    for o in range(1, planes):
        copy5(o, lax.rem(plane + o, planes)).wait_recv()

    for p in range(plan.pair):
        hidden = functools.reduce(
            jnp.add, [part_all[p * shorts + x] for x in range(shorts)]
        )
        rows = slice(p * answers, (p + 1) * answers)
        hidden_ref[p] = hidden
        both_ref[rows, :] = hidden
    hidden = both_ref[...]
    gain = jnp.broadcast_to(ffn_ref[...].astype(f32), hidden.shape)
    normed2_ref[...] = (hidden * gain).astype(bf16)
    high, low = split_two(
        jnp.broadcast_to(
            jnp.sum(hidden * hidden, axis=1, keepdims=True), (plan.all_answers, lane)
        )
    )
    square_ref[0] = high
    square_ref[1] = low

    many, folds = plan.all_answers, plan.folds

    def ffn_place(t, k):
        first = t // folds * lane + k * plan.half
        return slice(t % folds * many, (t % folds + 1) * many), slice(first, first + lane)

    def ffn_piece(i):
        for copy in ffn_copies(i):
            copy.wait()
        both = jnp.dot(
            normed2_ref[...], ffn_buf[i], preferred_element_type=f32
        )
        for k in range(2):
            mine = both[:, k * plan.piece : (k + 1) * plan.piece]
            for t, tile in enumerate(tiles_of(mine) + [square_ref[k]]):
                ffn_pack[ffn_place(t, k)] = tile
        ffn_send[i] = ffn_pack[...].astype(bf16)

    def copy6(i, source):
        return remote(
            ffn_send.at[i], ffn_recv.at[source], s6.at[i], r6.at[source], member(i)
        )

    def copy7(o, source):
        return remote(
            act.at[source], act.at[source], s7.at[o - 1], r7.at[source],
            member(lax.rem(me + o, n)),
        )

    def activate():
        total2 = ffn_send[me].astype(f32)
        for o in range(1, n):
            source = lax.rem(me + o, n)
            copy6(0, source).wait_recv()
            total2 += ffn_recv[source].astype(f32)
        ffn_sum[...] = total2
        square = ffn_sum[ffn_place(plan.tiles, 0)] + ffn_sum[ffn_place(plan.tiles, 1)]
        for g in range(folds):
            spread_ref[g * many : (g + 1) * many, :] = lax.rsqrt(square / plan.model + epsilon)
        factor2 = spread_ref[...]
        for t in range(plan.half // lane):
            gate = total2[:, t * lane : (t + 1) * lane] * factor2
            upward = total2[:, plan.half + t * lane : plan.half + (t + 1) * lane] * factor2
            act[me, :, t * lane : (t + 1) * lane] = (
                gate / (1.0 + jnp.exp(-gate)) * upward
            ).astype(bf16)
        for o in range(1, n):
            copy7(o, me).start()

    def ffn_step(i, carry):
        ffn_piece(i)

        @pl.when(me != i)
        def _():
            copy6(i, me).start()

        down_copy(i).start()
        pl.when(me == i - lag)(activate)
        return carry

    lax.fori_loop(0, owners, ffn_step, 0)

    wide_acc[...] = jnp.zeros_like(wide_acc)
    for j in range(owners):

        @pl.when(me != j)
        def _():
            copy7(1, j).wait_recv()

        down_copy(j).wait()
        block = act[j].astype(f32)
        for k in range(plan.tiles):
            first = (k // folds) * lane
            down_lhs[:, k * lane : (k + 1) * lane] = jnp.where(
                row16 // many == k % folds, block[:, first : first + lane], 0.0
            ).astype(bf16)
        wide_acc[...] += jnp.dot(
            down_lhs[...], down_buf[j * plan.piece : (j + 1) * plan.piece, :],
            preferred_element_type=f32,
        )
        if j == 0:
            pl.when(me == owners - 2)(activate)
        if j == 2:
            pl.when(me == owners - 1)(activate)
    both_ref[...] = folded(wide_acc[...], many)
    for p in range(plan.pair):
        last_part[p] = both_ref[p * answers : (p + 1) * answers, :]

    def copy8(o, source):
        target = lax.rem(plane + o, planes)
        return remote(
            last_part.at[target // shorts], last_recv.at[source], s8.at[o - 1], r8.at[source],
            in_plane(target),
        )

    for o in range(1, planes):
        copy8(o, plane).start()
    result = hidden_ref[part] + last_part[part]
    for o in range(1, planes):
        source = lax.rem(plane + o, planes)
        copy8(o, source).wait_recv()
        result += last_recv[source]
    out_ref[...] = result.astype(bf16)

    for o in range(1, wides):
        copy1(o).wait_send()
    for o in range(1, subs):
        copy2(o, sub).wait_send()
    for u in range(plan.units):

        @pl.when(me != u)
        def _():
            copy3(u, me).wait_send()

    @pl.when(me < plan.units)
    def _():
        for o in range(1, n):
            copy4(o, me).wait_send()

    for o in range(1, planes):
        copy5(o, plane).wait_send()
        copy8(o, plane).wait_send()
    for i in range(owners):

        @pl.when(me != i)
        def _():
            copy6(i, me).wait_send()

    @pl.when(me < owners)
    def _():
        for o in range(1, n):
            copy7(o, me).wait_send()


def per_device(
    sizes, residual, attn_gain, query_weight, key_value_weight, output_weight, cache_keys,
    cached_value_rows, lengths, positions, ffn_gain, gate_weight, up_weight, down_weight,
):
    plan = Plan(
        sizes, residual.shape, query_weight.shape, key_value_weight.shape, output_weight.shape,
        cache_keys.shape, gate_weight.shape, down_weight.shape,
    )
    n, answers = plan.members, plan.answers
    vmem = pl.BlockSpec(memory_space=pltpu.VMEM)
    smem = pl.BlockSpec(memory_space=pltpu.SMEM)
    hbm = pl.BlockSpec(memory_space=pltpu.HBM)
    dma = pltpu.SemaphoreType.DMA
    scratch = [
        pltpu.VMEM(query_weight.shape, bf16),
        pltpu.VMEM(key_value_weight.shape, bf16),
        pltpu.VMEM(output_weight.shape, bf16),
        pltpu.VMEM(cache_keys.shape, bf16),
        pltpu.VMEM(cache_keys.shape, bf16),
        pltpu.VMEM((plan.owners, plan.gate_rows, 2 * plan.piece), bf16),
        pltpu.VMEM((plan.ff, plan.out_cols), bf16),
        pltpu.VMEM((answers, plan.width), bf16),
        pltpu.VMEM((16, plan.pack_cols), f32),
        pltpu.VMEM((16, lane), f32),
        pltpu.VMEM((16, lane), f32),
        pltpu.VMEM((16, lane), f32),
        pltpu.VMEM((16, lane), f32),
        pltpu.VMEM((16, plan.pack_cols), bf16),
        pltpu.VMEM((plan.wide - 1, 16, plan.pack_cols), bf16),
        pltpu.VMEM((plan.sub, 16, plan.pack_cols), bf16),
        pltpu.VMEM((plan.units, 32, lane), bf16),
        pltpu.VMEM((n, 32, lane), bf16),
        pltpu.VMEM((plan.units, 16, lane), bf16),
        pltpu.VMEM((16, plan.out_rows), bf16),
        pltpu.VMEM((16, plan.out_cols), f32),
        pltpu.VMEM((plan.planes, answers, plan.out_cols), f32),
        pltpu.VMEM((plan.all_answers, plan.out_cols), bf16),
        pltpu.VMEM((plan.pair, answers, plan.out_cols), f32),
        pltpu.VMEM((plan.all_answers, plan.out_cols), f32),
        pltpu.VMEM((2, plan.all_answers, lane), f32),
        pltpu.VMEM((16, 2 * plan.half), f32),
        pltpu.VMEM((16, 2 * plan.half), f32),
        pltpu.VMEM((plan.owners, 16, 2 * plan.half), bf16),
        pltpu.VMEM((n, 16, 2 * plan.half), bf16),
        pltpu.VMEM((plan.owners, 16, plan.half), bf16),
        pltpu.VMEM((16, plan.piece), bf16),
        pltpu.VMEM((plan.pair, answers, plan.out_cols), f32),
        pltpu.VMEM((plan.planes, answers, plan.out_cols), f32),
        dma((plan.query_chunks,)),
        dma((1,)),
        dma((2,)),
        dma((plan.out_chunks,)),
        dma((plan.owners, 2)),
        dma((plan.owners,)),
        dma((plan.wide - 1,)), dma((plan.wide - 1,)),
        dma((plan.sub - 1,)), dma((plan.sub - 1,)),
        dma((plan.units,)), dma((n,)),
        dma((n - 1,)), dma((plan.units,)),
        dma((plan.planes,)), dma((plan.planes,)),
        dma((plan.owners,)), dma((n,)),
        dma((n - 1,)), dma((plan.owners,)),
        dma((plan.planes,)), dma((plan.planes,)),
    ]
    return pl.pallas_call(
        functools.partial(kernel, plan),
        out_shape=jax.ShapeDtypeStruct((answers, plan.out_cols), bf16),
        in_specs=[vmem, vmem, vmem, smem, smem] + [hbm] * 8,
        out_specs=vmem,
        scratch_shapes=scratch,
        compiler_params=pltpu.CompilerParams(
            collective_id=0, has_side_effects=True, vmem_limit_bytes=vmem_limit
        ),
        name="layer",
    )(
        residual, attn_gain, ffn_gain, lengths, positions,
        query_weight, key_value_weight, output_weight, cache_keys, cached_value_rows,
        gate_weight, up_weight, down_weight,
    )


def solution(mesh):
    sizes = tuple(mesh.shape[name] for name in ("wide", "short", "sub", "groups"))
    placed = (
        P("groups", "wide"),
        P("wide"),
        P("wide", ("short", "sub")),
        P("wide", ("short", "sub")),
        P("short", ("wide", "sub")),
        P("groups", "short", ("wide", "sub"), None),
        P("groups", "short", ("wide", "sub"), None),
        P("groups"),
        P("groups"),
        P(("wide", "sub")),
        P(("wide", "sub"), "short"),
        P(("wide", "sub"), "short"),
        P("short", ("wide", "sub")),
    )
    return jax.shard_map(
        functools.partial(per_device, sizes),
        mesh=mesh,
        in_specs=placed,
        out_specs=P("groups", ("wide", "sub")),
        check_vma=False,
    )
```

```python
import functools
import math

import jax
import jax.numpy as jnp
from jax import lax
from jax.experimental import pallas as pl
from jax.experimental.pallas import tpu as pltpu
from jax.sharding import PartitionSpec as P

rope_base = 1000000.0
epsilon = 1e-05
neg_large = -1e30
lane = 128
bf16 = jnp.bfloat16
f32 = jnp.float32
vmem_limit = 63 * 2**20


def split_two(value):
    high = value.astype(bf16).astype(f32)
    return high, value - high


def largest_divisor(count, most):
    return max(d for d in range(1, most + 1) if count % d == 0)


class Plan:
    def __init__(self, sizes, residual, query, keyval, output, cache, gate, down):
        self.wide, self.short, self.sub, self.pair = sizes
        self.members = self.wide * self.sub
        self.answers, self.width = residual
        self.groups = 16 // self.answers
        self.model = self.width * self.wide
        self.query_cols = query[1]
        self.heads = self.query_cols // lane
        self.blocks = keyval[1] // lane
        self.head_tiles = -(-self.heads // self.groups)
        self.pack_cols = -(-(self.heads + self.blocks + 2) // self.groups) * lane
        self.kv_heads = cache[1]
        self.rows = cache[2]
        self.units = self.sub * self.head_tiles
        self.out_rows, self.out_cols = output
        self.gate_rows, whole_ff = gate
        self.ff = whole_ff // self.pair
        self.all_answers = self.answers * self.pair
        self.folds = 16 // self.all_answers
        self.planes = self.pair * self.short
        self.owners = largest_divisor(self.ff // lane, self.members)
        self.piece = self.ff // self.owners
        self.tiles = self.piece // lane
        self.half = -(-(self.tiles + 1) // self.folds) * lane
        self.query_chunks = largest_divisor(self.width // lane, 6)
        self.out_chunks = largest_divisor(self.out_rows // lane, 6)
        assert self.members < 3 * self.owners and self.all_answers * self.folds == 16 and self.ff * self.pair == whole_ff
        assert self.units <= self.members and self.sub % self.kv_heads == 0
        assert self.blocks * self.sub == 2 * self.kv_heads


def kernel(
    plan,
    res_ref, attn_ref, ffn_ref, len_ref, pos_ref,
    query_hbm, keyval_hbm, output_hbm, keys_hbm, values_hbm, gate_hbm, up_hbm, down_hbm,
    out_ref,
    query_buf, keyval_buf, output_buf, keys_buf, values_buf, ffn_buf, down_buf,
    normed_ref, pack_ref, spread_ref, kv_ref, new_key_ref, new_value_ref,
    send1, recv1, rot, pay, recv_pay, att, out_lhs, wide_acc,
    part_all, normed2_ref, hidden_ref, both_ref, square_ref,
    ffn_pack, ffn_sum, ffn_send, ffn_recv, act, down_lhs, last_part, last_recv,
    query_sem, keyval_sem, cache_sem, output_sem, ffn_sem, down_sem,
    s1, r1, s2, r2, s3, r3, s4, r4, s5, r5, s6, r6, s7, r7, s8, r8,
):
    n, wides, shorts, subs = plan.members, plan.wide, plan.short, plan.sub
    answers, groups = plan.answers, plan.groups
    wide, short, sub = lax.axis_index("wide"), lax.axis_index("short"), lax.axis_index("sub")
    part = lax.axis_index("groups")
    planes = plan.planes
    plane = part * shorts + short
    me = wide * subs + sub
    owners = plan.owners

    def member(rank):
        return {"wide": rank // subs, "sub": rank % subs}

    def remote(src, dst, ssem, rsem, device):
        return pltpu.make_async_remote_copy(
            src_ref=src, dst_ref=dst, send_sem=ssem, recv_sem=rsem,
            device_id=device, device_id_type=pl.DeviceIdType.MESH,
        )

    barrier = pltpu.get_barrier_semaphore()
    for o in range(1, n):
        pl.semaphore_signal(
            barrier, inc=1, device_id=member(lax.rem(me + o, n)),
            device_id_type=pl.DeviceIdType.MESH,
        )
    def in_plane(rank):
        return {"groups": rank // shorts, "short": rank % shorts}

    for o in range(1, planes):
        pl.semaphore_signal(
            barrier, inc=1, device_id=in_plane(lax.rem(plane + o, planes)),
            device_id_type=pl.DeviceIdType.MESH,
        )

    q_rows = plan.width // plan.query_chunks
    o_rows = plan.out_rows // plan.out_chunks

    def query_copy(c):
        at = pl.ds(c * q_rows, q_rows)
        return pltpu.make_async_copy(query_hbm.at[at], query_buf.at[at], query_sem.at[c])

    def output_copy(c):
        at = pl.ds(c * o_rows, o_rows)
        return pltpu.make_async_copy(output_hbm.at[at], output_buf.at[at], output_sem.at[c])

    keyval_copy = pltpu.make_async_copy(keyval_hbm, keyval_buf, keyval_sem.at[0])
    keys_copy = pltpu.make_async_copy(keys_hbm, keys_buf, cache_sem.at[0])
    values_copy = pltpu.make_async_copy(values_hbm, values_buf, cache_sem.at[1])

    def ffn_owner(i):
        return lax.rem(me + 1 + i, owners)

    def down_owner(j):
        return lax.rem(me - j + 2 * owners, owners)

    def ffn_copies(i):
        first = part * plan.ff + ffn_owner(i) * plan.piece
        at = pl.ds(pl.multiple_of(first, lane), plan.piece)
        return [
            pltpu.make_async_copy(
                hbm.at[:, at],
                ffn_buf.at[i, :, pl.ds(k * plan.piece, plan.piece)],
                ffn_sem.at[i, k],
            )
            for k, hbm in enumerate((gate_hbm, up_hbm))
        ]

    def ffn_start(i):
        for copy in ffn_copies(i):
            copy.start()

    def down_copy(j):
        first = part * plan.ff + down_owner(j) * plan.piece
        at = pl.ds(pl.multiple_of(first, lane), plan.piece)
        here = pl.ds(pl.multiple_of(j * plan.piece, lane), plan.piece)
        return pltpu.make_async_copy(down_hbm.at[at], down_buf.at[here], down_sem.at[j])

    keyval_copy.start()
    for c in range(plan.query_chunks):
        query_copy(c).start()
    keys_copy.start()
    values_copy.start()
    begun = [0]

    def ffn_begin(sevenths):
        upto = -(-owners * sevenths // 7)
        for i in range(begun[0], upto):
            ffn_start(i)
        begun[0] = upto

    resid = res_ref[...].astype(f32)
    normed_ref[...] = (resid * attn_ref[...].astype(f32)).astype(bf16)
    squares = jnp.sum(resid * resid, axis=1, keepdims=True)

    row16 = lax.broadcasted_iota(jnp.int32, (16, lane), 0)
    lane16 = lax.broadcasted_iota(jnp.int32, (16, lane), 1)
    group16 = row16 // answers
    answer16 = row16 % answers
    position = jnp.zeros((16, lane), f32)
    for a in range(answers):
        position = jnp.where(answer16 == a, pos_ref[a].astype(f32), position)
    freq = jnp.exp((lane16 % (lane // 2)).astype(f32) * (-2.0 / lane * math.log(rope_base)))
    angle = position * freq
    cosine = jnp.cos(angle)
    sine = jnp.sin(angle)
    sine = jnp.where(lane16 < lane // 2, -sine, sine)
    ffn_pack[...] = jnp.zeros_like(ffn_pack)

    keyval_copy.wait()
    kv_part = jnp.dot(normed_ref[...], keyval_buf[...], preferred_element_type=f32)
    q_part = jnp.zeros((answers, plan.query_cols), f32)
    for c in range(plan.query_chunks):
        query_copy(c).wait()
        at = pl.ds(c * q_rows, q_rows)
        q_part += jnp.dot(normed_ref[:, at], query_buf[at, :], preferred_element_type=f32)
    def place(k):
        g, first = k % groups, k // groups * lane
        return slice(g * answers, (g + 1) * answers), slice(first, first + lane)

    def tiles_of(value):
        return [value[:, k * lane : (k + 1) * lane] for k in range(value.shape[1] // lane)]

    packed = tiles_of(q_part) + tiles_of(kv_part)
    packed += split_two(jnp.broadcast_to(squares, (answers, lane)))
    pack_ref[...] = jnp.zeros_like(pack_ref)
    for k, tile in enumerate(packed):
        pack_ref[place(k)] = tile
    send1[...] = pack_ref[...].astype(bf16)

    pl.semaphore_wait(barrier, n - 1 + planes - 1)

    def copy1(o):
        return remote(
            send1, recv1.at[o - 1], s1.at[o - 1], r1.at[o - 1],
            {"wide": lax.rem(wide + o, wides)},
        )

    for o in range(1, wides):
        copy1(o).start()
    for c in range(plan.out_chunks):
        output_copy(c).start()
    for o in range(1, wides):
        copy1(o).wait_recv()
        pack_ref[...] += recv1[o - 1].astype(f32)

    def spread(four):
        for g in range(groups):
            spread_ref[g * answers : (g + 1) * answers, :] = four
        return spread_ref[...]

    square_at = plan.heads + plan.blocks
    total = pack_ref[place(square_at)] + pack_ref[place(square_at + 1)]
    factor = spread(lax.rsqrt(total / plan.model + epsilon))
    for t in range(plan.pack_cols // lane):
        value = pack_ref[:, t * lane : (t + 1) * lane] * factor
        turned = value * cosine + pltpu.roll(value, lane // 2, 1) * sine
        if (t + 1) * groups > plan.heads:
            block = t * groups + group16 - plan.heads
            is_value = (block >= 0) & ((sub * plan.blocks + block + 2) % 2 == 1)
            turned = jnp.where(is_value, value, turned)
        rot[sub, :, t * lane : (t + 1) * lane] = turned.astype(bf16)

    def copy2(o, source):
        return remote(
            rot.at[source], rot.at[source], s2.at[o - 1], r2.at[o - 1],
            {"sub": lax.rem(sub + o, subs)},
        )

    for o in range(1, subs):
        copy2(o, sub).start()
    ffn_begin(1)
    for o in range(1, subs):
        copy2(o, lax.rem(sub - o + subs, subs)).wait_recv()

    keys_copy.wait()
    values_copy.wait()
    scaling = 1.0 / math.sqrt(lane)
    heads = plan.head_tiles
    sharers = subs // plan.kv_heads
    stacked = sharers * heads * 16
    row_id = lax.broadcasted_iota(jnp.int32, (stacked, plan.rows), 0)
    col_id = lax.broadcasted_iota(jnp.int32, (stacked, plan.rows), 1) + me * plan.rows
    valid = [(row_id % answers == a) & (col_id < len_ref[a]) for a in range(answers)]

    def copy3(u, source):
        return remote(pay.at[u], recv_pay.at[source], s3.at[u], r3.at[source], member(u))

    for h in range(plan.kv_heads):
        queries = jnp.concatenate(
            [
                rot[s, :, t * lane : (t + 1) * lane]
                for s in range(h * sharers, (h + 1) * sharers)
                for t in range(heads)
            ],
            axis=0,
        )
        for k, new_ref in enumerate((new_key_ref, new_value_ref)):
            block = 2 * h + k
            rows, columns = place(plan.heads + block % plan.blocks)
            kv_ref[...] = rot[block // plan.blocks, :, columns].astype(f32)
            for g in range(groups):
                new_ref[g * answers : (g + 1) * answers, :] = kv_ref[rows, :]
        new_key = jnp.concatenate([new_key_ref[...]] * (sharers * heads), axis=0)
        new_value = jnp.concatenate([new_value_ref[...]] * (sharers * heads), axis=0)
        own = jnp.sum(queries.astype(f32) * new_key, axis=1, keepdims=True) * scaling
        scores = []
        for a in range(answers):
            score = lax.dot_general(
                queries, keys_buf[a, h], (((1,), (1,)), ((), ())), preferred_element_type=f32
            )
            scores.append(jnp.where(valid[a], score * scaling, neg_large))
        top = functools.reduce(jnp.maximum, scores)
        top = jnp.max(top, axis=1, keepdims=True)
        top = jnp.where(me == 0, jnp.maximum(top, own), top)
        own_weight = jnp.where(me == 0, jnp.exp(own - top), 0.0)
        totals = own_weight
        mixed = own_weight * new_value
        for a in range(answers):
            weights = jnp.where(valid[a], jnp.exp(scores[a] - top), 0.0).astype(bf16)
            totals += jnp.sum(weights.astype(f32), axis=1, keepdims=True)
            mixed += jnp.dot(weights, values_buf[a, h], preferred_element_type=f32)
        for t in range(sharers * heads):
            u = h * sharers * heads + t
            rows = slice(t * 16, (t + 1) * 16)
            top_high, rest = split_two(jnp.broadcast_to(top[rows], (16, lane)))
            top_mid, top_low = split_two(rest)
            sum_high, sum_low = split_two(jnp.broadcast_to(totals[rows], (16, lane)))
            stats = jnp.where(lane16 < 64, sum_high, sum_low)
            stats = jnp.where(lane16 < 48, top_low, stats)
            stats = jnp.where(lane16 < 32, top_mid, stats)
            stats = jnp.where(lane16 < 16, top_high, stats)
            pay[u, :16, :] = mixed[rows].astype(bf16)
            pay[u, 16:, :] = stats.astype(bf16)

            @pl.when(me != u)
            def _():
                copy3(u, me).start()

    ffn_begin(3)

    def copy4(o, source):
        return remote(
            att.at[source], att.at[source], s4.at[o - 1], r4.at[source],
            member(lax.rem(me + o, n)),
        )

    @pl.when(me < plan.units)
    def _():
        parts = [pay[me].astype(f32)]
        for o in range(1, n):
            source = lax.rem(me + o, n)
            copy3(0, source).wait_recv()
            parts.append(recv_pay[source].astype(f32))
        tops = [
            p[16:, 0:1] + p[16:, 16:17] + p[16:, 32:33] for p in parts
        ]
        highest = functools.reduce(jnp.maximum, tops)
        numerator = jnp.zeros((16, lane), f32)
        denominator = jnp.zeros((16, 1), f32)
        for p, top in zip(parts, tops):
            scale = jnp.exp(top - highest)
            numerator += p[:16] * scale
            denominator += (p[16:, 48:49] + p[16:, 64:65]) * scale
        att[me] = (numerator / denominator).astype(bf16)
        for o in range(1, n):
            copy4(o, me).start()

    ffn_begin(5)
    for u in range(plan.units):

        @pl.when(me != u)
        def _():
            copy4(1, u).wait_recv()

    for u in range(plan.units):
        block = att[u].astype(f32)
        for g in range(groups):
            head = (u % heads) * groups + g
            if head >= plan.heads:
                continue
            head += u // heads * plan.heads
            out_lhs[:, head * lane : (head + 1) * lane] = jnp.where(
                group16 == g, block, 0.0
            ).astype(bf16)
    product = jnp.zeros((16, plan.out_cols), f32)
    for c in range(plan.out_chunks):
        output_copy(c).wait()
        at = pl.ds(c * o_rows, o_rows)
        product += jnp.dot(out_lhs[:, at], output_buf[at, :], preferred_element_type=f32)
    def folded(value, rows):
        wide_acc[...] = value
        return functools.reduce(
            jnp.add, [wide_acc[r : r + rows, :] for r in range(0, 16, rows)]
        )

    resid_part = res_ref[:, : plan.out_cols].astype(f32)
    for k in range(1, subs):
        here = res_ref[:, k * plan.out_cols : (k + 1) * plan.out_cols].astype(f32)
        resid_part = jnp.where(sub == k, here, resid_part)
    part_all[plane] = folded(product, answers) + jnp.where(short == 0, resid_part, 0.0)

    def copy5(o, source):
        return remote(
            part_all.at[source], part_all.at[source], s5.at[o - 1], r5.at[source],
            in_plane(lax.rem(plane + o, planes)),
        )

    for o in range(1, planes):
        copy5(o, plane).start()
    ffn_begin(7)
    for o in range(1, planes):
        copy5(o, lax.rem(plane + o, planes)).wait_recv()

    for p in range(plan.pair):
        hidden = functools.reduce(
            jnp.add, [part_all[p * shorts + x] for x in range(shorts)]
        )
        rows = slice(p * answers, (p + 1) * answers)
        hidden_ref[p] = hidden
        both_ref[rows, :] = hidden
    hidden = both_ref[...]
    gain = jnp.broadcast_to(ffn_ref[...].astype(f32), hidden.shape)
    normed2_ref[...] = (hidden * gain).astype(bf16)
    high, low = split_two(
        jnp.broadcast_to(
            jnp.sum(hidden * hidden, axis=1, keepdims=True), (plan.all_answers, lane)
        )
    )
    square_ref[0] = high
    square_ref[1] = low

    many, folds = plan.all_answers, plan.folds

    def ffn_place(t, k):
        first = t // folds * lane + k * plan.half
        return slice(t % folds * many, (t % folds + 1) * many), slice(first, first + lane)

    def ffn_piece(i):
        for copy in ffn_copies(i):
            copy.wait()
        both = jnp.dot(
            normed2_ref[...], ffn_buf[i], preferred_element_type=f32
        )
        for k in range(2):
            mine = both[:, k * plan.piece : (k + 1) * plan.piece]
            for t, tile in enumerate(tiles_of(mine) + [square_ref[k]]):
                ffn_pack[ffn_place(t, k)] = tile
        ffn_send[ffn_owner(i)] = ffn_pack[...].astype(bf16)

    def copy6(i, source):
        return remote(
            ffn_send.at[i], ffn_recv.at[source], s6.at[i], r6.at[source], member(i)
        )

    def copy7(o, source):
        return remote(
            act.at[source], act.at[source], s7.at[o - 1], r7.at[source],
            member(lax.rem(me + o, n)),
        )

    def activate():
        total2 = ffn_send[me].astype(f32)
        for o in range(1, n):
            source = lax.rem(me + o, n)
            copy6(0, source).wait_recv()
            total2 += ffn_recv[source].astype(f32)
        ffn_sum[...] = total2
        square = ffn_sum[ffn_place(plan.tiles, 0)] + ffn_sum[ffn_place(plan.tiles, 1)]
        for g in range(folds):
            spread_ref[g * many : (g + 1) * many, :] = lax.rsqrt(square / plan.model + epsilon)
        factor2 = spread_ref[...]
        for t in range(plan.half // lane):
            gate = total2[:, t * lane : (t + 1) * lane] * factor2
            upward = total2[:, plan.half + t * lane : plan.half + (t + 1) * lane] * factor2
            act[me, :, t * lane : (t + 1) * lane] = (
                gate / (1.0 + jnp.exp(-gate)) * upward
            ).astype(bf16)
        for o in range(1, n):
            copy7(o, me).start()

    def ffn_step(i, carry):
        ffn_piece(i)

        owner = ffn_owner(i)

        @pl.when(me != owner)
        def _():
            copy6(owner, me).start()

        down_copy(i).start()
        return carry

    lax.fori_loop(0, owners, ffn_step, 0)
    pl.when(me < owners)(activate)

    wide_acc[...] = jnp.zeros_like(wide_acc)
    for j in range(owners):
        owner = down_owner(j)

        @pl.when(me != owner)
        def _():
            copy7(1, owner).wait_recv()

        down_copy(j).wait()
        block = act[owner].astype(f32)
        for k in range(plan.tiles):
            first = (k // folds) * lane
            down_lhs[:, k * lane : (k + 1) * lane] = jnp.where(
                row16 // many == k % folds, block[:, first : first + lane], 0.0
            ).astype(bf16)
        wide_acc[...] += jnp.dot(
            down_lhs[...], down_buf[j * plan.piece : (j + 1) * plan.piece, :],
            preferred_element_type=f32,
        )
    both_ref[...] = folded(wide_acc[...], many)
    for p in range(plan.pair):
        last_part[p] = both_ref[p * answers : (p + 1) * answers, :]

    def copy8(o, source):
        target = lax.rem(plane + o, planes)
        return remote(
            last_part.at[target // shorts], last_recv.at[source], s8.at[o - 1], r8.at[source],
            in_plane(target),
        )

    for o in range(1, planes):
        copy8(o, plane).start()
    result = hidden_ref[part] + last_part[part]
    for o in range(1, planes):
        source = lax.rem(plane + o, planes)
        copy8(o, source).wait_recv()
        result += last_recv[source]
    out_ref[...] = result.astype(bf16)

    for o in range(1, wides):
        copy1(o).wait_send()
    for o in range(1, subs):
        copy2(o, sub).wait_send()
    for u in range(plan.units):

        @pl.when(me != u)
        def _():
            copy3(u, me).wait_send()

    @pl.when(me < plan.units)
    def _():
        for o in range(1, n):
            copy4(o, me).wait_send()

    for o in range(1, planes):
        copy5(o, plane).wait_send()
        copy8(o, plane).wait_send()
    for i in range(owners):

        @pl.when(me != i)
        def _():
            copy6(i, me).wait_send()

    @pl.when(me < owners)
    def _():
        for o in range(1, n):
            copy7(o, me).wait_send()


def per_device(
    sizes, residual, attn_gain, query_weight, key_value_weight, output_weight, cache_keys,
    cached_value_rows, lengths, positions, ffn_gain, gate_weight, up_weight, down_weight,
):
    plan = Plan(
        sizes, residual.shape, query_weight.shape, key_value_weight.shape, output_weight.shape,
        cache_keys.shape, gate_weight.shape, down_weight.shape,
    )
    n, answers = plan.members, plan.answers
    vmem = pl.BlockSpec(memory_space=pltpu.VMEM)
    smem = pl.BlockSpec(memory_space=pltpu.SMEM)
    hbm = pl.BlockSpec(memory_space=pltpu.HBM)
    dma = pltpu.SemaphoreType.DMA
    scratch = [
        pltpu.VMEM(query_weight.shape, bf16),
        pltpu.VMEM(key_value_weight.shape, bf16),
        pltpu.VMEM(output_weight.shape, bf16),
        pltpu.VMEM(cache_keys.shape, bf16),
        pltpu.VMEM(cache_keys.shape, bf16),
        pltpu.VMEM((plan.owners, plan.gate_rows, 2 * plan.piece), bf16),
        pltpu.VMEM((plan.ff, plan.out_cols), bf16),
        pltpu.VMEM((answers, plan.width), bf16),
        pltpu.VMEM((16, plan.pack_cols), f32),
        pltpu.VMEM((16, lane), f32),
        pltpu.VMEM((16, lane), f32),
        pltpu.VMEM((16, lane), f32),
        pltpu.VMEM((16, lane), f32),
        pltpu.VMEM((16, plan.pack_cols), bf16),
        pltpu.VMEM((plan.wide - 1, 16, plan.pack_cols), bf16),
        pltpu.VMEM((plan.sub, 16, plan.pack_cols), bf16),
        pltpu.VMEM((plan.units, 32, lane), bf16),
        pltpu.VMEM((n, 32, lane), bf16),
        pltpu.VMEM((plan.units, 16, lane), bf16),
        pltpu.VMEM((16, plan.out_rows), bf16),
        pltpu.VMEM((16, plan.out_cols), f32),
        pltpu.VMEM((plan.planes, answers, plan.out_cols), f32),
        pltpu.VMEM((plan.all_answers, plan.out_cols), bf16),
        pltpu.VMEM((plan.pair, answers, plan.out_cols), f32),
        pltpu.VMEM((plan.all_answers, plan.out_cols), f32),
        pltpu.VMEM((2, plan.all_answers, lane), f32),
        pltpu.VMEM((16, 2 * plan.half), f32),
        pltpu.VMEM((16, 2 * plan.half), f32),
        pltpu.VMEM((plan.owners, 16, 2 * plan.half), bf16),
        pltpu.VMEM((n, 16, 2 * plan.half), bf16),
        pltpu.VMEM((plan.owners, 16, plan.half), bf16),
        pltpu.VMEM((16, plan.piece), bf16),
        pltpu.VMEM((plan.pair, answers, plan.out_cols), f32),
        pltpu.VMEM((plan.planes, answers, plan.out_cols), f32),
        dma((plan.query_chunks,)),
        dma((1,)),
        dma((2,)),
        dma((plan.out_chunks,)),
        dma((plan.owners, 2)),
        dma((plan.owners,)),
        dma((plan.wide - 1,)), dma((plan.wide - 1,)),
        dma((plan.sub - 1,)), dma((plan.sub - 1,)),
        dma((plan.units,)), dma((n,)),
        dma((n - 1,)), dma((plan.units,)),
        dma((plan.planes,)), dma((plan.planes,)),
        dma((plan.owners,)), dma((n,)),
        dma((n - 1,)), dma((plan.owners,)),
        dma((plan.planes,)), dma((plan.planes,)),
    ]
    return pl.pallas_call(
        functools.partial(kernel, plan),
        out_shape=jax.ShapeDtypeStruct((answers, plan.out_cols), bf16),
        in_specs=[vmem, vmem, vmem, smem, smem] + [hbm] * 8,
        out_specs=vmem,
        scratch_shapes=scratch,
        compiler_params=pltpu.CompilerParams(
            collective_id=0, has_side_effects=True, vmem_limit_bytes=vmem_limit
        ),
        name="layer",
    )(
        residual, attn_gain, ffn_gain, lengths, positions,
        query_weight, key_value_weight, output_weight, cache_keys, cached_value_rows,
        gate_weight, up_weight, down_weight,
    )


def solution(mesh):
    sizes = tuple(mesh.shape[name] for name in ("wide", "short", "sub", "groups"))
    placed = (
        P("groups", "wide"),
        P("wide"),
        P("wide", ("short", "sub")),
        P("wide", ("short", "sub")),
        P("short", ("wide", "sub")),
        P("groups", "short", ("wide", "sub"), None),
        P("groups", "short", ("wide", "sub"), None),
        P("groups"),
        P("groups"),
        P(("wide", "sub")),
        P(("wide", "sub"), "short"),
        P(("wide", "sub"), "short"),
        P("short", ("wide", "sub")),
    )
    return jax.shard_map(
        functools.partial(per_device, sizes),
        mesh=mesh,
        in_specs=placed,
        out_specs=P("groups", ("wide", "sub")),
        check_vma=False,
    )
```
